32 devices in a mesh: groups: 2 (over y), samples: 4 (over z), views: 2 (over x), rhs: 2 (over core).
Axes of the slice: x: 2, y: 2, z: 4, core: 2. Of those that a mesh axis runs over, the one named last changes fastest.
Arguments:
- features: bfloat16 [8, 8192, 128], P('views', ('groups', 'samples')), parts along dimension 1, may hold values from -8 to 8
- kernel_inverse_scale: float32 [8], replicated, may hold values from 0.0078125 to 0.0234375
- view_weight: float32 [8], replicated, may hold values from 0.05 to 0.3
- ridge_term: float32 [16], P('rhs'), may hold values from 0.5 to 4
- solution: float32 [8192, 16], P(('groups', 'samples'), 'rhs'), parts along dimension 0, may hold values from -6 to 6
- residual: float32 [8192, 16], P(('groups', 'samples'), 'rhs'), parts along dimension 0, may hold values from -210 to 210
- direction: float32 [8192, 16], P(('groups', 'samples'), 'rhs'), parts along dimension 0, may hold values from -210 to 210
Outputs:
- solution_next: float32 [8192, 16], P(('groups', 'samples'), 'rhs'), parts along dimension 0
- residual_next: float32 [8192, 16], P(('groups', 'samples'), 'rhs'), parts along dimension 0
- direction_next: float32 [8192, 16], P(('groups', 'samples'), 'rhs'), parts along dimension 0
The draws below stay inside these ranges and needn't reach their ends.
There are 2 independent parts, one for each index of `groups`. The reference program is written for one: setup_inputs(seed, part) draws one part's arguments, and reference() takes and returns one part's arrays. A program takes and returns all parts, laid end to end along the dimension named above; an argument that names none is the same for every part. Nothing has to cross between parts.
All inputs are finite; a program needn't handle non-finite values.
Results may differ from the reference program's by a relative error of at most 0.0023.
Values may be sent and summed in bfloat16 or wider, within the bound.
A program may use at most 64 MiB of HBM per device.

```python
import math
import jax
import jax.numpy as jnp
from jax import lax

FEAT = 128
VIEWS = 8
RHS = 16
SAMPLES = 4096


def shaped(key, base, trend):
    key_row, key_col = jax.random.split(key)
    row_scale = jnp.exp(jax.random.uniform(key_row, (SAMPLES, 1), jnp.float32, 0.0, math.log(10.0)))
    col_scale = jnp.exp(jax.random.uniform(key_col, (1, RHS), jnp.float32, 0.0, math.log(4.0)))
    position = jnp.arange(SAMPLES, dtype=jnp.float32)[:, None] / max(SAMPLES - 1, 1)
    return base * row_scale * col_scale * jnp.exp(position * math.log(trend)) * 0.25


def draw_features(key, part):
    key = jax.random.fold_in(key, 37)
    subkeys = jax.random.split(key, 6)
    cluster_count = max(2, SAMPLES // 128)
    member = jax.random.randint(subkeys[0], (SAMPLES,), 0, cluster_count)
    spread = jnp.exp(jax.random.uniform(subkeys[1], (VIEWS, cluster_count, 1), jnp.float32, math.log(0.6), math.log(1.4)))
    centers = spread * jax.random.truncated_normal(subkeys[2], -4.0, 4.0, (VIEWS, cluster_count, FEAT), jnp.float32)
    latent = jax.random.truncated_normal(subkeys[4], -3.0, 3.0, (VIEWS, SAMPLES, 6), jnp.float32)
    jitter = 0.2 * jax.random.truncated_normal(subkeys[5], -4.0, 4.0, (VIEWS, SAMPLES, FEAT), jnp.float32)
    base_dirs = 0.5 * jax.random.truncated_normal(subkeys[3], -4.0, 4.0, (VIEWS, cluster_count, 6, FEAT), jnp.float32)
    placed = centers[:, member, :] + jitter
    for latent_dim in range(6):
        placed = placed + latent[:, :, latent_dim:latent_dim + 1] * base_dirs[:, member, latent_dim, :]
    return jnp.clip(placed, -8.0, 8.0).astype(jnp.bfloat16)


def draw_residual(key, part):
    key = jax.random.fold_in(key, 11)
    key_base, key_shape = jax.random.split(key)
    base = jax.random.truncated_normal(key_base, -4.0, 4.0, (SAMPLES, RHS), jnp.float32)
    return shaped(key_shape, base, 3.0)


def draw_direction(key, part):
    key = jax.random.fold_in(key, 23)
    key_base, key_shape = jax.random.split(key)
    base = jax.random.truncated_normal(key_base, -4.0, 4.0, (SAMPLES, RHS), jnp.float32)
    return shaped(key_shape, base, 3.0)


def block_scale(own_key, dims, cuts, low, top_value):
    level = 1.0
    for dim, blocks in cuts:
        draws = jax.random.uniform(jax.random.fold_in(jax.random.fold_in(own_key, 6), dim), (blocks,), jnp.float32, low / len(cuts), top_value / len(cuts))
        level = level * jnp.repeat(jnp.exp(draws), dims[dim] // blocks).reshape((-1,) + (1,) * (len(dims) - 1 - dim))
    return level


def centred(key, extent, width, reach, cuts=(), held_as=jnp.bfloat16):
    result = width * jax.random.normal(key, extent, jnp.float32)
    if cuts:
        result = result * block_scale(key, extent, cuts, -0.22, 0.18)
    return jnp.clip(result, -reach, reach).astype(held_as)


def setup_inputs(seed: int = 0, part: int = 0) -> dict:
    key_list = jax.random.split(jax.random.key(seed), 8)
    part_keys = jax.random.split(jax.random.fold_in(key_list[7], part), 8)
    features = draw_features(jax.random.fold_in(jax.random.fold_in(key_list[7], part), 71), part)
    kernel_inverse_scale = jnp.clip(jnp.exp(jax.random.uniform(key_list[1], (VIEWS,), jnp.float32, math.log(0.0078125), math.log(0.0234375))), 0.0078125, 0.0234375)
    view_weight = jnp.clip(jnp.exp(jax.random.uniform(key_list[2], (VIEWS,), jnp.float32, math.log(0.05), math.log(0.3))), 0.05, 0.3)
    ridge_term = jnp.clip(jnp.exp(math.log(4.0) - 2.0794415 * jax.random.uniform(key_list[3], (RHS,), jnp.float32) ** block_scale(key_list[3], (RHS,), ((0, 2),), -0.2, 0.2)), 0.5, 4.0)
    solution = centred(part_keys[4], (SAMPLES, RHS), 1.0, 6.0, ((0, 4), (1, 2)), jnp.float32)
    residual = draw_residual(jax.random.fold_in(jax.random.fold_in(key_list[7], part), 71), part)
    direction = draw_direction(jax.random.fold_in(jax.random.fold_in(key_list[7], part), 71), part)
    return dict(features=features, kernel_inverse_scale=kernel_inverse_scale, view_weight=view_weight, ridge_term=ridge_term, solution=solution, residual=residual, direction=direction)


FULL_PRECISION = lax.Precision.HIGHEST


def view_image(row_feats, every_feature, all_norms, scale_view, weight, low_dir):
    row_norms = jnp.sum(row_feats * row_feats, axis=-1)
    inner_rows = jnp.dot(row_feats, every_feature.T, precision=FULL_PRECISION)
    distance = row_norms[:, None] + all_norms[None, :] - 2.0 * inner_rows
    kernel = (weight * jnp.exp(-scale_view * distance)).astype(jnp.bfloat16)
    kernel = lax.optimization_barrier(kernel).astype(jnp.float32)
    return jnp.dot(kernel, low_dir, precision=FULL_PRECISION)


def reference(features, kernel_inverse_scale, view_weight, ridge_term, solution, residual, direction):
    full_feats = features.astype(jnp.float32)
    sq_norms = jnp.sum(full_feats * full_feats, axis=-1)
    low_dir = direction.astype(jnp.bfloat16)
    low_dir = lax.optimization_barrier(low_dir).astype(jnp.float32)
    row_block = math.gcd(SAMPLES, 1024)
    blocks = full_feats.reshape(VIEWS, SAMPLES // row_block, row_block, FEAT).transpose(1, 0, 2, 3)

    def one_block(row_group):
        def one_view(summed, pieces):
            row_feats, every_feature, all_norms, scale_view, weight = pieces
            return summed + view_image(row_feats, every_feature, all_norms, scale_view, weight, low_dir), None

        start_sum = jnp.zeros((row_block, RHS), jnp.float32)
        summed, _ = lax.scan(one_view, start_sum, (row_group, full_feats, sq_norms, kernel_inverse_scale, view_weight))
        return summed

    product = lax.map(one_block, blocks).reshape(SAMPLES, RHS)
    product = product + ridge_term[None, :] * direction
    norm_now = jnp.sum(residual * residual, axis=0)
    curvature = jnp.sum(direction * product, axis=0)
    step_size = norm_now / curvature
    solution_next = solution + step_size * direction
    residual_next = residual - step_size * product
    norm_next = jnp.sum(residual_next * residual_next, axis=0)
    direction_next = residual_next + (norm_next / norm_now) * direction
    return (solution_next, residual_next, direction_next)
```

```python
import functools
import math

import jax
import jax.numpy as jnp
from jax import lax
from jax.experimental import pallas as pl
from jax.experimental.pallas import tpu as pltpu
from jax.sharding import PartitionSpec as P

MESH = pl.DeviceIdType.MESH
LANES = (((1,), (1,)), ((), ()))


def cg_kernel(
    n, slots, tile,
    scale_ref, weight_ref, feats_ref, ridge_ref, sol_ref, res_ref, dir_ref,
    sol_out, res_out, dir_out,
    buf, dbuf, dpair, acc, ext_acc, norms, cout, cin, part, gath, stats,
    load_sem, fs, fr, ds, dr, ps, pr, cs, cr, es, er, gs, gr, ss, sr, dir_stage,
):
    z = lax.axis_index("samples")
    x = lax.axis_index("views")
    c = lax.axis_index("rhs")
    xs = lax.axis_size("views")
    local_views = feats_ref.shape[0]
    first_view = x * local_views
    rows = feats_ref.shape[1]
    half = local_views // 2

    if slots == 2:
        view = [c, half + c]
        sgn = [1, -1]
        pos = [z, n - 1 - z]
    else:
        view = [c]
        sgn = [1 - 2 * c]
        pos = [z * (1 - c) + (n - 1 - z) * c]

    def load(s):
        return pltpu.make_async_copy(feats_ref.at[view[s]], buf.at[s, 0], load_sem.at[s])

    for s in range(slots):
        load(s).start()

    barrier = pltpu.get_barrier_semaphore()
    peers = [{"samples": lax.rem(z + k, n)} for k in range(1, n)]
    cross = [(dx, dc) for dx in range(xs) for dc in range(2) if (dx, dc) != (0, 0)]
    peers += [{"views": lax.rem(x + dx, xs), "rhs": lax.rem(c + dc, 2)} for dx, dc in cross]
    for peer in peers:
        pl.semaphore_signal(barrier, inc=1, device_id=peer, device_id_type=MESH)
    pl.semaphore_wait(barrier, len(peers))

    def remote(src, dst, send, recv, target):
        return pltpu.make_async_remote_copy(
            src_ref=src, dst_ref=dst, send_sem=send, recv_sem=recv,
            device_id=target, device_id_type=MESH,
        )

    def ahead(s, steps):
        return {"samples": lax.rem(z + sgn[s] * steps + 2 * n, n)}

    def forward(s, d):
        return (
            remote(buf.at[s, d], buf.at[s, d + 1], fs.at[s, d], fr.at[s, d + 1], ahead(s, 1)),
            remote(dbuf.at[s, d], dbuf.at[s, d + 1], ds.at[s, d], dr.at[s, d + 1], ahead(s, 1)),
        )

    def back(s):
        return (
            remote(buf.at[s, 0], buf.at[s, n - 1], fs.at[s, n - 1], fr.at[s, n - 1], ahead(s, -1)),
            remote(dbuf.at[s, 0], dbuf.at[s, n - 1], ds.at[s, n - 1], dr.at[s, n - 1], ahead(s, -1)),
        )

    def give(s, d):
        return remote(cout.at[s, d], cin.at[s, d], cs.at[s, d], cr.at[s, d], ahead(s, -d))

    def give_end(s):
        return remote(ext_acc.at[s], cin.at[s, n - 1], es.at[s], cr.at[s, n - 1], ahead(s, 1))

    pair = remote(dir_ref, dpair.at[c], ps, pr, {"rhs": 1 - c})
    pair.start()
    stage = pltpu.make_async_copy(dir_ref, dpair.at[c], dir_stage)
    stage.start()
    for s in range(slots):
        load(s).wait()

        @pl.when(pos[s] < n - 1)
        def _(s=s):
            forward(s, 0)[0].start()

    stage.wait()
    pair.wait()
    low = jnp.concatenate([dpair[0], dpair[1]], axis=0).astype(jnp.bfloat16)
    for s in range(slots):
        dbuf[s, 0] = low

        @pl.when(pos[s] < n - 1)
        def _(s=s):
            forward(s, 0)[1].start()

    def consts(s):
        index = first_view + view[s]
        rate = scale_ref[index] * math.log2(math.e)
        return rate, jnp.log2(jnp.full((1, 1), weight_ref[index], jnp.float32))

    def row_term(s, slot_ref):
        rate, low_weight = consts(s)
        feats = slot_ref[...].astype(jnp.float32)
        sums = lax.dot_general(
            jnp.ones((8, feats.shape[1]), jnp.float32), feats * feats, LANES,
            precision=lax.Precision.HIGHEST, preferred_element_type=jnp.float32,
        )
        norms[s] = low_weight - rate * sums

    def block(s, jb, ib, jd, i_sum, j_sum, add_j):
        rate, _ = consts(s)

        def step(t, _):
            at = pl.ds(pl.multiple_of(t * tile, tile), tile)
            fj = jb[at, :]
            inner = lax.dot_general(fj, ib[...], LANES, preferred_element_type=jnp.float32)
            wide = fj.astype(jnp.float32)
            column = -rate * jnp.sum(wide * wide, axis=-1, keepdims=True)
            power = (2.0 * rate) * inner + norms[s, 0:1, :] + column
            kern = jnp.exp2(power).astype(jnp.bfloat16)
            i_sum[...] += jnp.dot(jd[:, at], kern, preferred_element_type=jnp.float32)
            if j_sum is not None:
                (idir, target) = j_sum
                term = lax.dot_general(idir[...], kern, LANES, preferred_element_type=jnp.float32)
                if add_j:
                    target[:, at] += term
                else:
                    target[:, at] = term
            return 0

        lax.fori_loop(0, rows // tile, step, 0)

    acc[...] = jnp.zeros_like(acc)
    for s in range(slots):
        row_term(s, buf.at[s, 0])
        block(s, buf.at[s, 0], buf.at[s, 0], dbuf.at[s, 0], acc, None, False)

    for s in range(slots):
        @pl.when(pos[s] == n - 1)
        def _(s=s):
            if slots == 2:
                forward(1 - s, 0)[0].wait_send()
            for copy in back(s):
                copy.start()

    def turn(d, _):
        for s in range(slots):
            @pl.when(pos[s] >= d)
            def _(s=s):
                for copy in forward(s, d - 1):
                    copy.wait_recv()

                @pl.when((pos[s] < n - 1) & (d < n - 2))
                def _():
                    for copy in forward(s, d):
                        copy.start()

                block(s, buf.at[s, d], buf.at[s, 0], dbuf.at[s, d], acc,
                      (dbuf.at[s, 0], cout.at[s, d]), False)

                @pl.when((pos[s] != n - 2) | (d != n - 2))
                def _():
                    give(s, d).start()
        return 0

    lax.fori_loop(1, n - 1, turn, 0)

    for s in range(slots):
        @pl.when(pos[s] == n - 2)
        def _(s=s):
            for copy in back(s):
                copy.wait_recv()
            row_term(s, buf.at[s, n - 1])
            ext_acc[s] = jnp.zeros(ext_acc.shape[1:], jnp.float32)
            block(s, buf.at[s, n - 2], buf.at[s, n - 1], dbuf.at[s, n - 2], ext_acc.at[s],
                  (dbuf.at[s, n - 1], cout.at[s, n - 2]), True)
            give_end(s).start()
            give(s, n - 2).start()

    def collect(d, _):
        for s in range(slots):
            @pl.when(pos[s] + d <= n - 1)
            def _(s=s):
                give(s, d).wait_recv()
                acc[...] += cin[s, d]
        return 0

    lax.fori_loop(1, n - 1, collect, 0)
    for s in range(slots):
        @pl.when(pos[s] == n - 1)
        def _(s=s):
            give_end(s).wait_recv()
            acc[...] += cin[s, n - 1]

    part[0] = acc[0:8, :]
    part[1] = acc[8:16, :]
    here = x * 2 + c

    def swap(k):
        dx, dc = cross[k]
        tx, tc = lax.rem(x + dx, xs), lax.rem(c + dc, 2)
        return remote(part.at[tc], gath.at[here], gs.at[k], gr.at[k], {"views": tx, "rhs": tc})

    for k in range(len(cross)):
        swap(k).start()
    gath[here] = part[c]
    for k in range(len(cross)):
        swap(k).wait()
    direction = dir_ref[...]
    residual = res_ref[...]
    summed = gath[0]
    for k in range(1, 2 * xs):
        summed = summed + gath[k]
    product = summed + ridge_ref[...] * direction

    def total(value):
        return jnp.sum(value, axis=-1, keepdims=True)

    lane = lax.broadcasted_iota(jnp.int32, (8, 128), 1)
    sums = jnp.zeros((8, 128), jnp.float32)
    for k, value in enumerate((residual * residual, direction * product,
                               residual * product, product * product)):
        sums = jnp.where(lane == k, total(value), sums)
    stats[z] = sums

    def spread(k):
        return remote(stats.at[z], stats.at[z], ss.at[k], sr.at[k], {"samples": lax.rem(z + k, n)})

    for k in range(1, n):
        spread(k).start()
    for k in range(1, n):
        spread(k).wait()
    sums = stats[0]
    for k in range(1, n):
        sums = sums + stats[k]
    norm_now, curvature, cross_term, square = (sums[:, k:k + 1] for k in range(4))
    step_size = norm_now / curvature
    norm_next = jnp.maximum(norm_now - step_size * (2.0 * cross_term - step_size * square), 0.0)
    sol_out[...] = sol_ref[...] + step_size * direction
    residual_next = residual - step_size * product
    res_out[...] = residual_next
    dir_out[...] = residual_next + norm_next / norm_now * direction

    for s in range(slots):
        @pl.when(pos[s] < n - 1)
        def _(s=s):
            if slots == 2:
                @pl.when(pos[1 - s] != n - 1)
                def _():
                    forward(s, 0)[0].wait_send()
            else:
                forward(s, 0)[0].wait_send()
            forward(s, 0)[1].wait_send()

        @pl.when(pos[s] == n - 1)
        def _(s=s):
            for copy in back(s):
                copy.wait_send()

        @pl.when(pos[s] == n - 2)
        def _(s=s):
            give_end(s).wait_send()

    def drain(d, _):
        for s in range(slots):
            @pl.when(pos[s] >= d)
            def _(s=s):
                give(s, d).wait_send()

                @pl.when((pos[s] < n - 1) & (d < n - 2))
                def _():
                    for copy in forward(s, d):
                        copy.wait_send()
        return 0

    lax.fori_loop(1, n - 1, drain, 0)


def per_device(
    features, kernel_inverse_scale, view_weight, ridge_term, solution, residual, direction
):
    n = lax.axis_size("samples")
    xs = lax.axis_size("views")
    local_views, rows, feat = features.shape
    cols = direction.shape[1]
    slots = local_views // 2
    tile = math.gcd(rows, 256)
    vmem = pl.BlockSpec(memory_space=pltpu.VMEM)
    smem = pl.BlockSpec(memory_space=pltpu.SMEM)
    dma = pltpu.SemaphoreType.DMA
    f32, bf16 = jnp.float32, jnp.bfloat16
    out = jax.ShapeDtypeStruct((cols, rows), f32)
    outs = pl.pallas_call(
        functools.partial(cg_kernel, n, slots, tile),
        out_shape=(out, out, out),
        in_specs=[smem, smem, pl.BlockSpec(memory_space=pl.ANY), vmem, vmem, vmem, vmem],
        out_specs=(vmem, vmem, vmem),
        scratch_shapes=[
            pltpu.VMEM((slots, n, rows, feat), bf16),
            pltpu.VMEM((slots, n, 2 * cols, rows), bf16),
            pltpu.VMEM((2, cols, rows), f32),
            pltpu.VMEM((2 * cols, rows), f32),
            pltpu.VMEM((slots, 2 * cols, rows), f32),
            pltpu.VMEM((slots, 8, rows), f32),
            pltpu.VMEM((slots, n, 2 * cols, rows), f32),
            pltpu.VMEM((slots, n, 2 * cols, rows), f32),
            pltpu.VMEM((2, cols, rows), f32),
            pltpu.VMEM((2 * xs, cols, rows), f32),
            pltpu.VMEM((n, cols, 128), f32),
            dma((slots,)),
            dma((slots, n)), dma((slots, n)),
            dma((slots, n)), dma((slots, n)),
            dma, dma,
            dma((slots, n)), dma((slots, n)),
            dma((slots,)), dma((slots,)),
            dma((2 * xs - 1,)), dma((2 * xs - 1,)),
            dma((n,)), dma((n,)),
            dma,
        ],
        compiler_params=pltpu.CompilerParams(
            collective_id=0, has_side_effects=True, vmem_limit_bytes=48 * 1024 * 1024
        ),
    )(
        kernel_inverse_scale, view_weight, features, ridge_term[:, None],
        solution.T, residual.T, direction.T,
    )
    return tuple(value.T for value in outs)


def solution(mesh):
    return jax.shard_map(
        per_device,
        mesh=mesh,
        in_specs=(
            P("views", ("groups", "samples"), None),
            P(),
            P(),
            P("rhs"),
            P(("groups", "samples"), "rhs"),
            P(("groups", "samples"), "rhs"),
            P(("groups", "samples"), "rhs"),
        ),
        out_specs=(
            P(("groups", "samples"), "rhs"),
            P(("groups", "samples"), "rhs"),
            P(("groups", "samples"), "rhs"),
        ),
        check_vma=False,
    )
```

```python
import functools
import math

import jax
import jax.numpy as jnp
from jax import lax
from jax.experimental import pallas as pl
from jax.experimental.pallas import tpu as pltpu
from jax.sharding import PartitionSpec as P

MESH = pl.DeviceIdType.MESH
LANES = (((1,), (1,)), ((), ()))


def cg_kernel(
    n, slots, tile,
    scale_hbm, weight_hbm, ridge_hbm, feats_ref, res_hbm, dir_hbm,
    product_out, step_out, ratio_out,
    scale_ref, weight_ref, ridge_ref, res_ref,
    buf, dbuf, dpair, acc, ext_acc, norms, cout, cin, part, gath, stats,
    load_sem, small_sem, fs, fr, ds, dr, ps, pr, cs, cr, es, gs, gr, ss, sr,
):
    z = lax.axis_index("samples")
    x = lax.axis_index("views")
    c = lax.axis_index("rhs")
    xs = lax.axis_size("views")
    local_views = feats_ref.shape[0]
    first_view = x * local_views
    rows = feats_ref.shape[1]
    half = local_views // 2
    pieces = [pl.ds(k * tile, tile) for k in range(rows // tile)]

    if slots == 2:
        view = [c, half + c]
        sgn = [1, -1]
        pos = [z, n - 1 - z]
    else:
        view = [c]
        sgn = [1 - 2 * c]
        pos = [z * (1 - c) + (n - 1 - z) * c]

    def load(s):
        return pltpu.make_async_copy(feats_ref.at[view[s]], buf.at[s, 0], load_sem.at[s])

    fetch = [
        pltpu.make_async_copy(src, dst, small_sem.at[k])
        for k, (src, dst) in enumerate((
            (dir_hbm, dpair.at[c]), (scale_hbm, scale_ref), (weight_hbm, weight_ref),
            (ridge_hbm, ridge_ref), (res_hbm, res_ref),
        ))
    ]
    for s in range(slots):
        load(s).start()
    for copy in fetch:
        copy.start()

    barrier = pltpu.get_barrier_semaphore()
    peers = [{"samples": lax.rem(z + k, n)} for k in range(1, n)]
    cross = [(dx, dc) for dx in range(xs) for dc in range(2) if (dx, dc) != (0, 0)]
    peers += [{"views": lax.rem(x + dx, xs), "rhs": lax.rem(c + dc, 2)} for dx, dc in cross]
    for peer in peers:
        pl.semaphore_signal(barrier, inc=1, device_id=peer, device_id_type=MESH)
    pl.semaphore_wait(barrier, len(peers))

    def remote(src, dst, send, recv, target):
        return pltpu.make_async_remote_copy(
            src_ref=src, dst_ref=dst, send_sem=send, recv_sem=recv,
            device_id=target, device_id_type=MESH,
        )

    def ahead(s, steps):
        return {"samples": lax.rem(z + sgn[s] * steps + 2 * n, n)}

    def forward(s, d):
        return tuple(
            remote(buf.at[s, d, at], buf.at[s, d + 1, at],
                   fs.at[s, d, k], fr.at[s, d + 1, k], ahead(s, 1))
            for k, at in enumerate(pieces)
        ) + (
            remote(dbuf.at[s, d], dbuf.at[s, d + 1], ds.at[s, d], dr.at[s, d + 1], ahead(s, 1)),
        )

    def back(s):
        return tuple(
            remote(buf.at[s, 0, at], buf.at[s, n - 1, at],
                   fs.at[s, n - 1, k], fr.at[s, n - 1, k], ahead(s, -1))
            for k, at in enumerate(pieces)
        ) + (
            remote(dbuf.at[s, 0], dbuf.at[s, n - 1], ds.at[s, n - 1], dr.at[s, n - 1], ahead(s, -1)),
        )

    def give(s, d):
        return remote(cout.at[s, d], cin.at[s, d], cs.at[s, d], cr.at[s, d], ahead(s, -d))

    def give_end(s):
        return remote(ext_acc.at[s], cin.at[s, n - 1], es.at[s], cr.at[s, n - 1], ahead(s, 1))

    for copy in fetch:
        copy.wait()
    pair = remote(dpair.at[c], dpair.at[c], ps, pr, {"rhs": 1 - c})
    pair.start()
    for s in range(slots):
        load(s).wait()

        @pl.when(pos[s] < n - 1)
        def _(s=s):
            for copy in forward(s, 0)[:-1]:
                copy.start()

    pair.wait()
    low = jnp.concatenate([dpair[0], dpair[1]], axis=0).astype(jnp.bfloat16)
    for s in range(slots):
        dbuf[s, 0] = low

        @pl.when(pos[s] < n - 1)
        def _(s=s):
            forward(s, 0)[-1].start()

    def consts(s):
        index = first_view + view[s]
        rate = scale_ref[index] * math.log2(math.e)
        return rate, jnp.log2(jnp.full((1, 1), weight_ref[index], jnp.float32))

    def row_term(s, slot_ref):
        rate, low_weight = consts(s)
        feats = slot_ref[...].astype(jnp.float32)
        sums = lax.dot_general(
            jnp.ones((8, feats.shape[1]), jnp.float32), feats * feats, LANES,
            precision=lax.Precision.HIGHEST, preferred_element_type=jnp.float32,
        )
        norms[s] = low_weight - rate * sums

    def block(s, jb, ib, jd, at, i_sum, j_sum, add_j):
        rate, _ = consts(s)
        fj = jb[at, :]
        inner = lax.dot_general(fj, ib[...], LANES, preferred_element_type=jnp.float32)
        wide = fj.astype(jnp.float32)
        column = -rate * jnp.sum(wide * wide, axis=-1, keepdims=True)
        power = (2.0 * rate) * inner + norms[s, 0:1, :] + column
        kern = jnp.exp2(power).astype(jnp.bfloat16)
        i_sum[...] += jnp.dot(jd[:, at], kern, preferred_element_type=jnp.float32)
        if j_sum is not None:
            (idir, target) = j_sum
            term = lax.dot_general(idir[...], kern, LANES, preferred_element_type=jnp.float32)
            if add_j:
                target[:, at] += term
            else:
                target[:, at] = term

    def each_piece(run):
        def step(t, _):
            run(pl.ds(pl.multiple_of(t * tile, tile), tile))
            return 0

        lax.fori_loop(0, rows // tile, step, 0)

    acc[...] = jnp.zeros_like(acc)
    for s in range(slots):
        row_term(s, buf.at[s, 0])
        each_piece(functools.partial(
            lambda s, at: block(s, buf.at[s, 0], buf.at[s, 0], dbuf.at[s, 0], at, acc, None, False),
            s))

    for s in range(slots):
        @pl.when(pos[s] == n - 1)
        def _(s=s):
            if slots == 2:
                for copy in forward(1 - s, 0)[:-1]:
                    copy.wait_send()
            for copy in back(s):
                copy.start()

    def turn(d, _):
        for k, at in enumerate(pieces):
            for s in range(slots):
                @pl.when(pos[s] >= d)
                def _(s=s, k=k, at=at):
                    forward(s, d - 1)[k].wait_recv()

                    @pl.when((pos[s] < n - 1) & (d < n - 2))
                    def _():
                        forward(s, d)[k].start()

                    if k == 0:
                        forward(s, d - 1)[-1].wait_recv()

                        @pl.when((pos[s] < n - 1) & (d < n - 2))
                        def _():
                            forward(s, d)[-1].start()

                    block(s, buf.at[s, d], buf.at[s, 0], dbuf.at[s, d], at, acc,
                          (dbuf.at[s, 0], cout.at[s, d]), False)

                    if k == len(pieces) - 1:
                        @pl.when((pos[s] != n - 2) | (d != n - 2))
                        def _():
                            give(s, d).start()
        return 0

    lax.fori_loop(1, n - 1, turn, 0)

    for s in range(slots):
        @pl.when(pos[s] == n - 2)
        def _(s=s):
            for copy in back(s):
                copy.wait_recv()
            row_term(s, buf.at[s, n - 1])
            ext_acc[s] = jnp.zeros(ext_acc.shape[1:], jnp.float32)
            each_piece(lambda at: block(
                s, buf.at[s, n - 2], buf.at[s, n - 1], dbuf.at[s, n - 2], at, ext_acc.at[s],
                (dbuf.at[s, n - 1], cout.at[s, n - 2]), True))
            give_end(s).start()
            give(s, n - 2).start()

    def collect(d, _):
        for s in range(slots):
            @pl.when(pos[s] + d <= n - 1)
            def _(s=s):
                give(s, d).wait_recv()
                acc[...] += cin[s, d]
        return 0

    lax.fori_loop(1, n - 1, collect, 0)
    for s in range(slots):
        @pl.when(pos[s] == n - 1)
        def _(s=s):
            give_end(s).wait_recv()
            acc[...] += cin[s, n - 1]

    part[0] = acc[0:8, :]
    part[1] = acc[8:16, :]
    here = x * 2 + c

    def swap(k):
        dx, dc = cross[k]
        tx, tc = lax.rem(x + dx, xs), lax.rem(c + dc, 2)
        return remote(part.at[tc], gath.at[here], gs.at[k], gr.at[k], {"views": tx, "rhs": tc})

    for k in range(len(cross)):
        swap(k).start()
    gath[here] = part[c]
    for k in range(len(cross)):
        swap(k).wait()
    direction = dpair[c]
    residual = res_ref[...]
    summed = gath[0]
    for k in range(1, 2 * xs):
        summed = summed + gath[k]
    row = lax.broadcasted_iota(jnp.int32, (8, 1), 0)
    ridge = jnp.zeros((8, 1), jnp.float32)
    for k in range(8):
        ridge = jnp.where(row == k, ridge_ref[k], ridge)
    product = summed + ridge * direction
    product_out[...] = product

    def total(value):
        return jnp.sum(value, axis=-1, keepdims=True)

    lane = lax.broadcasted_iota(jnp.int32, (8, 128), 1)
    sums = jnp.zeros((8, 128), jnp.float32)
    for k, value in enumerate((residual * residual, direction * product,
                               residual * product, product * product)):
        sums = jnp.where(lane == k, total(value), sums)
    stats[z] = sums

    def spread(k):
        return remote(stats.at[z], stats.at[z], ss.at[k], sr.at[k], {"samples": lax.rem(z + k, n)})

    for k in range(1, n):
        spread(k).start()
    for k in range(1, n):
        spread(k).wait()
    sums = stats[0]
    for k in range(1, n):
        sums = sums + stats[k]
    norm_now, curvature, cross_term, square = (sums[:, k:k + 1] for k in range(4))
    step_size = norm_now / curvature
    norm_next = jnp.maximum(norm_now - step_size * (2.0 * cross_term - step_size * square), 0.0)
    step_out[...] = jnp.broadcast_to(step_size, step_out.shape)
    ratio_out[...] = jnp.broadcast_to(norm_next / norm_now, ratio_out.shape)

    for s in range(slots):
        @pl.when(pos[s] < n - 1)
        def _(s=s):
            if slots == 2:
                @pl.when(pos[1 - s] != n - 1)
                def _():
                    for copy in forward(s, 0)[:-1]:
                        copy.wait_send()
            else:
                for copy in forward(s, 0)[:-1]:
                    copy.wait_send()
            forward(s, 0)[-1].wait_send()

        @pl.when(pos[s] == n - 1)
        def _(s=s):
            for copy in back(s):
                copy.wait_send()

        @pl.when(pos[s] == n - 2)
        def _(s=s):
            give_end(s).wait_send()

    def drain(d, _):
        for s in range(slots):
            @pl.when(pos[s] >= d)
            def _(s=s):
                give(s, d).wait_send()

                @pl.when((pos[s] < n - 1) & (d < n - 2))
                def _():
                    for copy in forward(s, d):
                        copy.wait_send()
        return 0

    lax.fori_loop(1, n - 1, drain, 0)


def per_device(
    features, kernel_inverse_scale, view_weight, ridge_term, solution, residual, direction
):
    n = lax.axis_size("samples")
    xs = lax.axis_size("views")
    local_views, rows, feat = features.shape
    cols = direction.shape[1]
    slots = local_views // 2
    tile = math.gcd(rows, 512)
    chunks = rows // tile
    vmem = pl.BlockSpec(memory_space=pltpu.VMEM)
    hbm = pl.BlockSpec(memory_space=pltpu.HBM)
    dma = pltpu.SemaphoreType.DMA
    f32, bf16 = jnp.float32, jnp.bfloat16
    out = jax.ShapeDtypeStruct((cols, rows), f32)
    product, step_size, ratio = pl.pallas_call(
        functools.partial(cg_kernel, n, slots, tile),
        out_shape=(out, out, out),
        in_specs=[hbm] * 6,
        out_specs=(vmem, vmem, vmem),
        scratch_shapes=[
            pltpu.SMEM(kernel_inverse_scale.shape, f32),
            pltpu.SMEM(view_weight.shape, f32),
            pltpu.SMEM(ridge_term.shape, f32),
            pltpu.VMEM((cols, rows), f32),
            pltpu.VMEM((slots, n, rows, feat), bf16),
            pltpu.VMEM((slots, n, 2 * cols, rows), bf16),
            pltpu.VMEM((2, cols, rows), f32),
            pltpu.VMEM((2 * cols, rows), f32),
            pltpu.VMEM((slots, 2 * cols, rows), f32),
            pltpu.VMEM((slots, 8, rows), f32),
            pltpu.VMEM((slots, n, 2 * cols, rows), f32),
            pltpu.VMEM((slots, n, 2 * cols, rows), f32),
            pltpu.VMEM((2, cols, rows), f32),
            pltpu.VMEM((2 * xs, cols, rows), f32),
            pltpu.VMEM((n, cols, 128), f32),
            dma((slots,)),
            dma((5,)),
            dma((slots, n, chunks)), dma((slots, n, chunks)),
            dma((slots, n)), dma((slots, n)),
            dma, dma,
            dma((slots, n)), dma((slots, n)),
            dma((slots,)),
            dma((2 * xs - 1,)), dma((2 * xs - 1,)),
            dma((n,)), dma((n,)),
        ],
        compiler_params=pltpu.CompilerParams(
            collective_id=0, has_side_effects=True, vmem_limit_bytes=63 * 1024 * 1024
        ),
    )(
        kernel_inverse_scale, view_weight, ridge_term, features, residual.T, direction.T,
    )
    product, step_size, ratio = product.T, step_size.T, ratio.T
    solution_next = solution + step_size * direction
    residual_next = residual - step_size * product
    direction_next = residual_next + ratio * direction
    return (solution_next, residual_next, direction_next)


def solution(mesh):
    return jax.shard_map(
        per_device,
        mesh=mesh,
        in_specs=(
            P("views", ("groups", "samples"), None),
            P(),
            P(),
            P("rhs"),
            P(("groups", "samples"), "rhs"),
            P(("groups", "samples"), "rhs"),
            P(("groups", "samples"), "rhs"),
        ),
        out_specs=(
            P(("groups", "samples"), "rhs"),
            P(("groups", "samples"), "rhs"),
            P(("groups", "samples"), "rhs"),
        ),
        check_vma=False,
    )
```

```python
import functools
import math

import jax
import jax.numpy as jnp
from jax import lax
from jax.experimental import pallas as pl
from jax.experimental.pallas import tpu as pltpu
from jax.sharding import PartitionSpec as P

MESH = pl.DeviceIdType.MESH
LANES = (((1,), (1,)), ((), ()))


def cg_kernel(
    n, slots, tile,
    scale_hbm, weight_hbm, ridge_hbm, feats_ref, res_hbm, dir_hbm,
    product_out, step_out, ratio_out,
    scale_ref, weight_ref, ridge_ref, res_ref,
    buf, dbuf, dpair, acc, ext_acc, norms, cout, cin, part, gath, tot, stats,
    load_sem, small_sem, fs, fr, ds, dr, ps, pr, cs, cr, es, gs, gr, ss, sr,
):
    z = lax.axis_index("samples")
    x = lax.axis_index("views")
    c = lax.axis_index("rhs")
    xs = lax.axis_size("views")
    local_views = feats_ref.shape[0]
    first_view = x * local_views
    rows = feats_ref.shape[1]
    half = local_views // 2
    pieces = [pl.ds(k * tile, tile) for k in range(rows // tile)]

    if slots == 2:
        view = [c, half + c]
        sgn = [1, -1]
        pos = [z, n - 1 - z]
    else:
        view = [c]
        sgn = [1 - 2 * c]
        pos = [z * (1 - c) + (n - 1 - z) * c]

    def load(s):
        return pltpu.make_async_copy(feats_ref.at[view[s]], buf.at[s, 0], load_sem.at[s])

    fetch = [
        pltpu.make_async_copy(src, dst, small_sem.at[k])
        for k, (src, dst) in enumerate((
            (dir_hbm, dpair.at[c]), (scale_hbm, scale_ref), (weight_hbm, weight_ref),
            (ridge_hbm, ridge_ref), (res_hbm, res_ref),
        ))
    ]
    for s in range(slots):
        load(s).start()
    for copy in fetch:
        copy.start()

    barrier = pltpu.get_barrier_semaphore()
    sides = (z > 0).astype(jnp.int32) + (z < n - 1).astype(jnp.int32)
    cross = [(dx, dc) for dx in range(xs) for dc in range(2) if (dx, dc) != (0, 0)]
    for near, there in ((z - 1, z > 0), (z + 1, z < n - 1)):
        @pl.when(there)
        def _(near=near):
            pl.semaphore_signal(
                barrier, inc=1, device_id={"samples": near}, device_id_type=MESH)
    for dx, dc in cross:
        pl.semaphore_signal(
            barrier, inc=1, device_id_type=MESH,
            device_id={"views": lax.rem(x + dx, xs), "rhs": lax.rem(c + dc, 2)})
    pl.semaphore_wait(barrier, len(cross) + sides)

    def remote(src, dst, send, recv, target):
        return pltpu.make_async_remote_copy(
            src_ref=src, dst_ref=dst, send_sem=send, recv_sem=recv,
            device_id=target, device_id_type=MESH,
        )

    def ahead(s, steps):
        return {"samples": lax.rem(z + sgn[s] * steps + 2 * n, n)}

    def forward(s, d):
        return tuple(
            remote(buf.at[s, d, at], buf.at[s, d + 1, at],
                   fs.at[s, d, k], fr.at[s, d + 1, k], ahead(s, 1))
            for k, at in enumerate(pieces)
        ) + (
            remote(dbuf.at[s, d], dbuf.at[s, d + 1], ds.at[s, d], dr.at[s, d + 1], ahead(s, 1)),
        )

    def back(s):
        return tuple(
            remote(buf.at[s, 0, at], buf.at[s, n - 1, at],
                   fs.at[s, n - 1, k], fr.at[s, n - 1, k], ahead(s, -1))
            for k, at in enumerate(pieces)
        ) + (
            remote(dbuf.at[s, 0], dbuf.at[s, n - 1], ds.at[s, n - 1], dr.at[s, n - 1], ahead(s, -1)),
        )

    here = x * 2 + c
    owners = [(dx, oc) for dx in range(xs) for oc in range(2)]

    def give(s, d, k):
        return [
            remote(cout.at[s, d, pl.ds(8 * oc, 8), pieces[k]], cin.at[s, d, here, :, pieces[k]],
                   cs.at[s, d, k, j], cr.at[s, d, k, here],
                   {"views": lax.rem(x + dx, xs), "rhs": oc} | ahead(s, -d))
            for j, (dx, oc) in enumerate(owners)
        ]

    def give_end(s):
        return [
            remote(ext_acc.at[s, pl.ds(8 * oc, 8)], cin.at[s, n - 1, here],
                   es.at[s, j], cr.at[s, n - 1, 0, here],
                   {"views": lax.rem(x + dx, xs), "rhs": oc} | ahead(s, 1))
            for j, (dx, oc) in enumerate(owners)
        ]

    def taken(s, d, k, source):
        at = pieces[k] if d is not None else pl.ds(0, rows)
        d = n - 1 if d is None else d
        return remote(cout.at[s, d, pl.ds(0, 8), at], cin.at[s, d, source, :, at],
                      cs.at[s, d, k, 0], cr.at[s, d, k, source], ahead(s, 1))

    for copy in fetch:
        copy.wait()
    pair = remote(dpair.at[c], dpair.at[c], ps, pr, {"rhs": 1 - c})
    pair.start()
    for s in range(slots):
        load(s).wait()

        @pl.when(pos[s] < n - 1)
        def _(s=s):
            for copy in forward(s, 0)[:-1]:
                copy.start()

    pair.wait()
    low = jnp.concatenate([dpair[0], dpair[1]], axis=0).astype(jnp.bfloat16)
    for s in range(slots):
        dbuf[s, 0] = low

        @pl.when(pos[s] < n - 1)
        def _(s=s):
            forward(s, 0)[-1].start()

    def consts(s):
        index = first_view + view[s]
        rate = scale_ref[index] * math.log2(math.e)
        return rate, jnp.log2(jnp.full((1, 1), weight_ref[index], jnp.float32))

    def row_term(s, slot_ref):
        rate, low_weight = consts(s)
        feats = slot_ref[...].astype(jnp.float32)
        sums = lax.dot_general(
            jnp.ones((8, feats.shape[1]), jnp.float32), feats * feats, LANES,
            precision=lax.Precision.HIGHEST, preferred_element_type=jnp.float32,
        )
        norms[s] = low_weight - rate * sums

    def block(s, jb, ib, jd, at, i_sum, j_sum, add_j):
        rate, _ = consts(s)
        fj = jb[at, :]
        inner = lax.dot_general(fj, ib[...], LANES, preferred_element_type=jnp.float32)
        wide = fj.astype(jnp.float32)
        column = -rate * jnp.sum(wide * wide, axis=-1, keepdims=True)
        power = (2.0 * rate) * inner + norms[s, 0:1, :] + column
        kern = jnp.exp2(power).astype(jnp.bfloat16)
        i_sum[...] += jnp.dot(jd[:, at], kern, preferred_element_type=jnp.float32)
        if j_sum is not None:
            (idir, target) = j_sum
            term = lax.dot_general(idir[...], kern, LANES, preferred_element_type=jnp.float32)
            if add_j:
                target[:, at] += term
            else:
                target[:, at] = term

    def each_piece(run):
        def step(t, _):
            run(pl.ds(pl.multiple_of(t * tile, tile), tile))
            return 0

        lax.fori_loop(0, rows // tile, step, 0)

    acc[...] = jnp.zeros_like(acc)
    for s in range(slots):
        row_term(s, buf.at[s, 0])
        each_piece(functools.partial(
            lambda s, at: block(s, buf.at[s, 0], buf.at[s, 0], dbuf.at[s, 0], at, acc, None, False),
            s))

    for s in range(slots):
        @pl.when(pos[s] == n - 1)
        def _(s=s):
            moves = back(s)
            moves[-1].start()
            for k in range(len(pieces)):
                if slots == 2:
                    forward(1 - s, 0)[k].wait_send()
                moves[k].start()

    def turn(d, _):
        for k, at in enumerate(pieces):
            for s in range(slots):
                @pl.when(pos[s] >= d)
                def _(s=s, k=k, at=at):
                    forward(s, d - 1)[k].wait_recv()

                    @pl.when((pos[s] < n - 1) & (d < n - 2))
                    def _():
                        forward(s, d)[k].start()

                    if k == 0:
                        forward(s, d - 1)[-1].wait_recv()

                        @pl.when((pos[s] < n - 1) & (d < n - 2))
                        def _():
                            forward(s, d)[-1].start()

                    block(s, buf.at[s, d], buf.at[s, 0], dbuf.at[s, d], at, acc,
                          (dbuf.at[s, 0], cout.at[s, d]), False)

                    @pl.when((pos[s] != n - 2) | (d != n - 2))
                    def _():
                        for copy in give(s, d, k):
                            copy.start()
        return 0

    lax.fori_loop(1, n - 1, turn, 0)

    for s in range(slots):
        @pl.when(pos[s] == n - 2)
        def _(s=s):
            for copy in back(s):
                copy.wait_recv()
            row_term(s, buf.at[s, n - 1])
            ext_acc[s] = jnp.zeros(ext_acc.shape[1:], jnp.float32)
            for k, at in enumerate(pieces):
                block(s, buf.at[s, n - 2], buf.at[s, n - 1], dbuf.at[s, n - 2], at, ext_acc.at[s],
                      (dbuf.at[s, n - 1], cout.at[s, n - 2]), True)
                for copy in give(s, n - 2, k):
                    copy.start()
            for copy in give_end(s):
                copy.start()

    part[0] = acc[0:8, :]
    part[1] = acc[8:16, :]

    def swap(k):
        dx, dc = cross[k]
        tx, tc = lax.rem(x + dx, xs), lax.rem(c + dc, 2)
        return remote(part.at[tc], gath.at[here], gs.at[k], gr.at[k], {"views": tx, "rhs": tc})

    for k in range(len(cross)):
        swap(k).start()
    gath[here] = part[c]

    def place(s, core):
        return pos[s] if slots == 2 else z * (1 - core) + (n - 1 - z) * core

    for k in range(len(cross)):
        swap(k).wait()
    direction = dpair[c]
    residual = res_ref[...]
    summed = gath[0]
    for k in range(1, 2 * xs):
        summed = summed + gath[k]
    tot[...] = summed

    def collect(d, _):
        for s in range(slots):
            for core in range(2):
                @pl.when(place(s, core) + d <= n - 1)
                def _(s=s, core=core):
                    for other in range(xs):
                        source = other * 2 + core
                        for k in range(len(pieces)):
                            taken(s, d, k, source).wait_recv()
                        tot[...] += cin[s, d, source]
        return 0

    lax.fori_loop(1, n - 1, collect, 0)
    for s in range(slots):
        for core in range(2):
            @pl.when(place(s, core) == n - 1)
            def _(s=s, core=core):
                for other in range(xs):
                    source = other * 2 + core
                    taken(s, None, 0, source).wait_recv()
                    tot[...] += cin[s, n - 1, source]
    summed = tot[...]
    row = lax.broadcasted_iota(jnp.int32, (8, 1), 0)
    ridge = jnp.zeros((8, 1), jnp.float32)
    for k in range(8):
        ridge = jnp.where(row == k, ridge_ref[k], ridge)
    product = summed + ridge * direction
    product_out[...] = product

    def total(value):
        return jnp.sum(value, axis=-1, keepdims=True)

    lane = lax.broadcasted_iota(jnp.int32, (8, 128), 1)
    sums = jnp.zeros((8, 128), jnp.float32)
    for k, value in enumerate((residual * residual, direction * product,
                               residual * product, product * product)):
        sums = jnp.where(lane == k, total(value), sums)
    stats[z] = sums

    def spread(k):
        return remote(stats.at[z], stats.at[z], ss.at[k], sr.at[k], {"samples": lax.rem(z + k, n)})

    for k in range(1, n):
        spread(k).start()
    for k in range(1, n):
        spread(k).wait()
    sums = stats[0]
    for k in range(1, n):
        sums = sums + stats[k]
    norm_now, curvature, cross_term, square = (sums[:, k:k + 1] for k in range(4))
    step_size = norm_now / curvature
    norm_next = jnp.maximum(norm_now - step_size * (2.0 * cross_term - step_size * square), 0.0)
    step_out[...] = jnp.broadcast_to(step_size, step_out.shape)
    ratio_out[...] = jnp.broadcast_to(norm_next / norm_now, ratio_out.shape)

    for s in range(slots):
        @pl.when(pos[s] < n - 1)
        def _(s=s):
            if slots == 2:
                @pl.when(pos[1 - s] != n - 1)
                def _():
                    for copy in forward(s, 0)[:-1]:
                        copy.wait_send()
            else:
                for copy in forward(s, 0)[:-1]:
                    copy.wait_send()
            forward(s, 0)[-1].wait_send()

        @pl.when(pos[s] == n - 1)
        def _(s=s):
            for copy in back(s):
                copy.wait_send()

        @pl.when(pos[s] == n - 2)
        def _(s=s):
            for copy in give_end(s):
                copy.wait_send()

    def drain(d, _):
        for s in range(slots):
            @pl.when(pos[s] >= d)
            def _(s=s):
                for k in range(len(pieces)):
                    for copy in give(s, d, k):
                        copy.wait_send()

                @pl.when((pos[s] < n - 1) & (d < n - 2))
                def _():
                    for copy in forward(s, d):
                        copy.wait_send()
        return 0

    lax.fori_loop(1, n - 1, drain, 0)


def per_device(
    features, kernel_inverse_scale, view_weight, ridge_term, solution, residual, direction
):
    n = lax.axis_size("samples")
    xs = lax.axis_size("views")
    local_views, rows, feat = features.shape
    cols = direction.shape[1]
    slots = local_views // 2
    tile = math.gcd(rows, 512)
    chunks = rows // tile
    vmem = pl.BlockSpec(memory_space=pltpu.VMEM)
    hbm = pl.BlockSpec(memory_space=pltpu.HBM)
    dma = pltpu.SemaphoreType.DMA
    f32, bf16 = jnp.float32, jnp.bfloat16
    out = jax.ShapeDtypeStruct((cols, rows), f32)
    product, step_size, ratio = pl.pallas_call(
        functools.partial(cg_kernel, n, slots, tile),
        out_shape=(out, out, out),
        in_specs=[hbm] * 6,
        out_specs=(vmem, vmem, vmem),
        scratch_shapes=[
            pltpu.SMEM(kernel_inverse_scale.shape, f32),
            pltpu.SMEM(view_weight.shape, f32),
            pltpu.SMEM(ridge_term.shape, f32),
            pltpu.VMEM((cols, rows), f32),
            pltpu.VMEM((slots, n, rows, feat), bf16),
            pltpu.VMEM((slots, n, 2 * cols, rows), bf16),
            pltpu.VMEM((2, cols, rows), f32),
            pltpu.VMEM((2 * cols, rows), f32),
            pltpu.VMEM((slots, 2 * cols, rows), f32),
            pltpu.VMEM((slots, 8, rows), f32),
            pltpu.VMEM((slots, n, 2 * cols, rows), f32),
            pltpu.VMEM((slots, n, 2 * xs, cols, rows), f32),
            pltpu.VMEM((2, cols, rows), f32),
            pltpu.VMEM((2 * xs, cols, rows), f32),
            pltpu.VMEM((cols, rows), f32),
            pltpu.VMEM((n, cols, 128), f32),
            dma((slots,)),
            dma((5,)),
            dma((slots, n, chunks)), dma((slots, n, chunks)),
            dma((slots, n)), dma((slots, n)),
            dma, dma,
            dma((slots, n, chunks, 2 * xs)), dma((slots, n, chunks, 2 * xs)),
            dma((slots, 2 * xs)),
            dma((2 * xs - 1,)), dma((2 * xs - 1,)),
            dma((n,)), dma((n,)),
        ],
        compiler_params=pltpu.CompilerParams(
            collective_id=0, has_side_effects=True, vmem_limit_bytes=63 * 1024 * 1024
        ),
    )(
        kernel_inverse_scale, view_weight, ridge_term, features, residual.T, direction.T,
    )
    product, step_size, ratio = product.T, step_size.T, ratio.T
    solution_next = solution + step_size * direction
    residual_next = residual - step_size * product
    direction_next = residual_next + ratio * direction
    return (solution_next, residual_next, direction_next)


def solution(mesh):
    return jax.shard_map(
        per_device,
        mesh=mesh,
        in_specs=(
            P("views", ("groups", "samples"), None),
            P(),
            P(),
            P("rhs"),
            P(("groups", "samples"), "rhs"),
            P(("groups", "samples"), "rhs"),
            P(("groups", "samples"), "rhs"),
        ),
        out_specs=(
            P(("groups", "samples"), "rhs"),
            P(("groups", "samples"), "rhs"),
            P(("groups", "samples"), "rhs"),
        ),
        check_vma=False,
    )
```

```python
import functools
import math

import jax
import jax.numpy as jnp
from jax import lax
from jax.experimental import pallas as pl
from jax.experimental.pallas import tpu as pltpu
from jax.sharding import PartitionSpec as P

MESH = pl.DeviceIdType.MESH
LANES = (((1,), (1,)), ((), ()))


def cg_kernel(
    n, slots, tile,
    scale_hbm, weight_hbm, ridge_hbm, feats_ref, res_hbm, dir_hbm,
    product_out, step_out, ratio_out,
    scale_ref, weight_ref, ridge_ref, res_ref,
    buf, dbuf, dpair, acc, ext_acc, norms, norms_end, cout, cin, late, part, gath, tot, stats,
    load_sem, small_sem, fs, fr, ds, dr, ps, pr, cs, cr, ls, lr, gs, gr, ss, sr,
):
    z = lax.axis_index("samples")
    x = lax.axis_index("views")
    c = lax.axis_index("rhs")
    xs = lax.axis_size("views")
    local_views = feats_ref.shape[0]
    first_view = x * local_views
    rows = feats_ref.shape[1]
    half = local_views // 2
    pieces = [pl.ds(k * tile, tile) for k in range(rows // tile)]

    if slots == 2:
        view = [c, half + c]
        sgn = [1, -1]
        pos = [z, n - 1 - z]
    else:
        view = [c]
        sgn = [1 - 2 * c]
        pos = [z * (1 - c) + (n - 1 - z) * c]

    def load(s):
        return pltpu.make_async_copy(feats_ref.at[view[s]], buf.at[s, 0], load_sem.at[s])

    fetch = [
        pltpu.make_async_copy(src, dst, small_sem.at[k])
        for k, (src, dst) in enumerate((
            (dir_hbm, dpair.at[c]), (scale_hbm, scale_ref), (weight_hbm, weight_ref),
            (ridge_hbm, ridge_ref), (res_hbm, res_ref),
        ))
    ]
    for s in range(slots):
        load(s).start()
    for copy in fetch:
        copy.start()

    barrier = pltpu.get_barrier_semaphore()
    sides = (z > 0).astype(jnp.int32) + (z < n - 1).astype(jnp.int32)
    cross = [(dx, dc) for dx in range(xs) for dc in range(2) if (dx, dc) != (0, 0)]
    for near, there in ((z - 1, z > 0), (z + 1, z < n - 1)):
        @pl.when(there)
        def _(near=near):
            pl.semaphore_signal(
                barrier, inc=1, device_id={"samples": near}, device_id_type=MESH)
    for dx, dc in cross:
        pl.semaphore_signal(
            barrier, inc=1, device_id_type=MESH,
            device_id={"views": lax.rem(x + dx, xs), "rhs": lax.rem(c + dc, 2)})
    pl.semaphore_wait(barrier, len(cross) + sides)

    def remote(src, dst, send, recv, target):
        return pltpu.make_async_remote_copy(
            src_ref=src, dst_ref=dst, send_sem=send, recv_sem=recv,
            device_id=target, device_id_type=MESH,
        )

    def ahead(s, steps):
        return {"samples": lax.rem(z + sgn[s] * steps + 2 * n, n)}

    def forward(s, d):
        return tuple(
            remote(buf.at[s, d, at], buf.at[s, d + 1, at],
                   fs.at[s, d, k], fr.at[s, d + 1, k], ahead(s, 1))
            for k, at in enumerate(pieces)
        ) + (
            remote(dbuf.at[s, d], dbuf.at[s, d + 1], ds.at[s, d], dr.at[s, d + 1], ahead(s, 1)),
        )

    def back(s):
        return tuple(
            remote(buf.at[s, 0, at], buf.at[s, n - 1, at],
                   fs.at[s, n - 1, k], fr.at[s, n - 1, k], ahead(s, -1))
            for k, at in enumerate(pieces)
        ) + (
            remote(dbuf.at[s, 0], dbuf.at[s, n - 1], ds.at[s, n - 1], dr.at[s, n - 1], ahead(s, -1)),
        )

    here = x * 2 + c
    owners = [(dx, oc) for dx in range(xs) for oc in range(2)]

    def give(s, d, k):
        return remote(cout.at[s, d, :, pieces[k]], cin.at[s, d, :, pieces[k]],
                      cs.at[s, d, k], cr.at[s, d, k], ahead(s, -d))

    def give_last(s, k):
        return [
            remote(cout.at[s, n - 2, pl.ds(8 * oc, 8), pieces[k]],
                   late.at[s, 0, here, :, pieces[k]],
                   ls.at[s, 0, k, j], lr.at[s, 0, k, here],
                   {"views": lax.rem(x + dx, xs), "rhs": oc} | ahead(s, 2 - n))
            for j, (dx, oc) in enumerate(owners)
        ]

    def give_end(s):
        return [
            remote(ext_acc.at[s, pl.ds(8 * oc, 8)], late.at[s, 1, here],
                   ls.at[s, 1, 0, j], lr.at[s, 1, 0, here],
                   {"views": lax.rem(x + dx, xs), "rhs": oc} | ahead(s, 1))
            for j, (dx, oc) in enumerate(owners)
        ]

    def taken(s, e, k, source):
        at = pl.ds(0, rows) if e else pieces[k]
        return remote(cout.at[s, n - 2, pl.ds(0, 8), at], late.at[s, e, source, :, at],
                      ls.at[s, e, k, 0], lr.at[s, e, k, source], ahead(s, 1))

    for copy in fetch:
        copy.wait()
    pair = remote(dpair.at[c], dpair.at[c], ps, pr, {"rhs": 1 - c})
    pair.start()
    for s in range(slots):
        load(s).wait()

        @pl.when(pos[s] < n - 1)
        def _(s=s):
            for copy in forward(s, 0)[:-1]:
                copy.start()

    pair.wait()
    low = jnp.concatenate([dpair[0], dpair[1]], axis=0).astype(jnp.bfloat16)
    for s in range(slots):
        dbuf[s, 0] = low

        @pl.when(pos[s] < n - 1)
        def _(s=s):
            forward(s, 0)[-1].start()

    def consts(s):
        index = first_view + view[s]
        rate = scale_ref[index] * math.log2(math.e)
        return rate, jnp.log2(jnp.full((1, 1), weight_ref[index], jnp.float32))

    def row_term(s, slot_ref, norms):
        rate, low_weight = consts(s)
        feats = slot_ref[...].astype(jnp.float32)
        sums = lax.dot_general(
            jnp.ones((8, feats.shape[1]), jnp.float32), feats * feats, LANES,
            precision=lax.Precision.HIGHEST, preferred_element_type=jnp.float32,
        )
        norms[s] = low_weight - rate * sums

    def block(s, jb, ib, jd, at, i_sum, j_sum, add_j, norms):
        rate, _ = consts(s)
        fj = jb[at, :]
        inner = lax.dot_general(fj, ib[...], LANES, preferred_element_type=jnp.float32)
        wide = fj.astype(jnp.float32)
        column = -rate * jnp.sum(wide * wide, axis=-1, keepdims=True)
        power = (2.0 * rate) * inner + norms[s, 0:1, :] + column
        kern = jnp.exp2(power).astype(jnp.bfloat16)
        i_sum[...] += jnp.dot(jd[:, at], kern, preferred_element_type=jnp.float32)
        if j_sum is not None:
            (idir, target) = j_sum
            term = lax.dot_general(idir[...], kern, LANES, preferred_element_type=jnp.float32)
            if add_j:
                target[:, at] += term
            else:
                target[:, at] = term

    def each_piece(run):
        def step(t, _):
            run(pl.ds(pl.multiple_of(t * tile, tile), tile))
            return 0

        lax.fori_loop(0, rows // tile, step, 0)

    acc[...] = jnp.zeros_like(acc)
    for s in range(slots):
        row_term(s, buf.at[s, 0], norms)
        each_piece(functools.partial(
            lambda s, at: block(s, buf.at[s, 0], buf.at[s, 0], dbuf.at[s, 0], at, acc, None, False,
                                norms),
            s))

    for s in range(slots):
        @pl.when(pos[s] == n - 1)
        def _(s=s):
            moves = back(s)
            moves[-1].start()
            for k in range(len(pieces)):
                if slots == 2:
                    forward(1 - s, 0)[k].wait_send()
                moves[k].start()

    def end_piece(s, k):
        if k == 0:
            for copy in back(s):
                copy.wait_recv()
            row_term(s, buf.at[s, n - 1], norms_end)
            ext_acc[s] = jnp.zeros(ext_acc.shape[1:], jnp.float32)
        block(s, buf.at[s, n - 2], buf.at[s, n - 1], dbuf.at[s, n - 2], pieces[k], ext_acc.at[s],
              (dbuf.at[s, n - 1], cout.at[s, n - 2]), True, norms_end)
        for copy in give_last(s, k):
            copy.start()

    def turn(d, _):
        for k, at in enumerate(pieces):
            for s in range(slots):
                @pl.when(pos[s] >= d)
                def _(s=s, k=k):
                    forward(s, d - 1)[k].wait_recv()

                    @pl.when((pos[s] < n - 1) & (d < n - 2))
                    def _():
                        forward(s, d)[k].start()

                    if k == 0:
                        forward(s, d - 1)[-1].wait_recv()

                        @pl.when((pos[s] < n - 1) & (d < n - 2))
                        def _():
                            forward(s, d)[-1].start()

            for s in range(slots):
                @pl.when(pos[s] >= d)
                def _(s=s, k=k, at=at):
                    block(s, buf.at[s, d], buf.at[s, 0], dbuf.at[s, d], at, acc,
                          (dbuf.at[s, 0], cout.at[s, d]), False, norms)

                    @pl.when(d < n - 2)
                    def _():
                        give(s, d, k).start()

                    @pl.when((pos[s] == n - 1) & (d == n - 2))
                    def _():
                        for copy in give_last(s, k):
                            copy.start()

                    if k < len(pieces) - 1:
                        @pl.when((pos[s] == n - 2) & (d == n - 2))
                        def _():
                            end_piece(s, k)
        return 0

    lax.fori_loop(1, n - 1, turn, 0)

    def collect(d, _):
        for s in range(slots):
            @pl.when(pos[s] + d <= n - 1)
            def _(s=s):
                for k in range(len(pieces)):
                    give(s, d, k).wait_recv()
                acc[...] += cin[s, d]
        return 0

    lax.fori_loop(1, n - 2, collect, 0)

    part[0] = acc[0:8, :]
    part[1] = acc[8:16, :]

    def swap(k):
        dx, dc = cross[k]
        tx, tc = lax.rem(x + dx, xs), lax.rem(c + dc, 2)
        return remote(part.at[tc], gath.at[here], gs.at[k], gr.at[k], {"views": tx, "rhs": tc})

    for k in range(len(cross)):
        swap(k).start()
    gath[here] = part[c]

    for s in range(slots):
        @pl.when(pos[s] == n - 2)
        def _(s=s):
            end_piece(s, len(pieces) - 1)
            for copy in give_end(s):
                copy.start()


    def place(s, core):
        return pos[s] if slots == 2 else z * (1 - core) + (n - 1 - z) * core

    for k in range(len(cross)):
        swap(k).wait()
    direction = dpair[c]
    residual = res_ref[...]
    summed = gath[0]
    for k in range(1, 2 * xs):
        summed = summed + gath[k]
    tot[...] = summed

    for s in range(slots):
        for core in range(2):
            for e in range(2):
                @pl.when((place(s, core) <= 1) if e == 0 else (place(s, core) == n - 1))
                def _(s=s, core=core, e=e):
                    for other in range(xs):
                        source = other * 2 + core
                        for k in range(1 if e else len(pieces)):
                            taken(s, e, k, source).wait_recv()
                        tot[...] += late[s, e, source]
    summed = tot[...]
    row = lax.broadcasted_iota(jnp.int32, (8, 1), 0)
    ridge = jnp.zeros((8, 1), jnp.float32)
    for k in range(8):
        ridge = jnp.where(row == k, ridge_ref[k], ridge)
    product = summed + ridge * direction
    product_out[...] = product

    def total(value):
        return jnp.sum(value, axis=-1, keepdims=True)

    lane = lax.broadcasted_iota(jnp.int32, (8, 128), 1)
    sums = jnp.zeros((8, 128), jnp.float32)
    for k, value in enumerate((residual * residual, direction * product,
                               residual * product, product * product)):
        sums = jnp.where(lane == k, total(value), sums)
    stats[z] = sums

    def spread(k):
        return remote(stats.at[z], stats.at[z], ss.at[k], sr.at[k], {"samples": lax.rem(z + k, n)})

    for k in range(1, n):
        spread(k).start()
    for k in range(1, n):
        spread(k).wait()
    sums = stats[0]
    for k in range(1, n):
        sums = sums + stats[k]
    norm_now, curvature, cross_term, square = (sums[:, k:k + 1] for k in range(4))
    step_size = norm_now / curvature
    norm_next = jnp.maximum(norm_now - step_size * (2.0 * cross_term - step_size * square), 0.0)
    step_out[...] = jnp.broadcast_to(step_size, step_out.shape)
    ratio_out[...] = jnp.broadcast_to(norm_next / norm_now, ratio_out.shape)

    for s in range(slots):
        @pl.when(pos[s] < n - 1)
        def _(s=s):
            if slots == 2:
                @pl.when(pos[1 - s] != n - 1)
                def _():
                    for copy in forward(s, 0)[:-1]:
                        copy.wait_send()
            else:
                for copy in forward(s, 0)[:-1]:
                    copy.wait_send()
            forward(s, 0)[-1].wait_send()

        @pl.when(pos[s] == n - 1)
        def _(s=s):
            for copy in back(s):
                copy.wait_send()

        @pl.when(pos[s] == n - 2)
        def _(s=s):
            for copy in give_end(s):
                copy.wait_send()

    def drain(d, _):
        for s in range(slots):
            @pl.when(pos[s] >= d)
            def _(s=s):
                for k in range(len(pieces)):
                    @pl.when(d < n - 2)
                    def _(k=k):
                        give(s, d, k).wait_send()

                    @pl.when(d == n - 2)
                    def _(k=k):
                        for copy in give_last(s, k):
                            copy.wait_send()

                @pl.when((pos[s] < n - 1) & (d < n - 2))
                def _():
                    for copy in forward(s, d):
                        copy.wait_send()
        return 0

    lax.fori_loop(1, n - 1, drain, 0)


def per_device(
    features, kernel_inverse_scale, view_weight, ridge_term, solution, residual, direction
):
    n = lax.axis_size("samples")
    xs = lax.axis_size("views")
    local_views, rows, feat = features.shape
    cols = direction.shape[1]
    slots = local_views // 2
    tile = math.gcd(rows, 512)
    chunks = rows // tile
    vmem = pl.BlockSpec(memory_space=pltpu.VMEM)
    hbm = pl.BlockSpec(memory_space=pltpu.HBM)
    dma = pltpu.SemaphoreType.DMA
    f32, bf16 = jnp.float32, jnp.bfloat16
    out = jax.ShapeDtypeStruct((cols, rows), f32)
    product, step_size, ratio = pl.pallas_call(
        functools.partial(cg_kernel, n, slots, tile),
        out_shape=(out, out, out),
        in_specs=[hbm] * 6,
        out_specs=(vmem, vmem, vmem),
        scratch_shapes=[
            pltpu.SMEM(kernel_inverse_scale.shape, f32),
            pltpu.SMEM(view_weight.shape, f32),
            pltpu.SMEM(ridge_term.shape, f32),
            pltpu.VMEM((cols, rows), f32),
            pltpu.VMEM((slots, n, rows, feat), bf16),
            pltpu.VMEM((slots, n, 2 * cols, rows), bf16),
            pltpu.VMEM((2, cols, rows), f32),
            pltpu.VMEM((2 * cols, rows), f32),
            pltpu.VMEM((slots, 2 * cols, rows), f32),
            pltpu.VMEM((slots, 8, rows), f32),
            pltpu.VMEM((slots, 8, rows), f32),
            pltpu.VMEM((slots, n, 2 * cols, rows), f32),
            pltpu.VMEM((slots, n, 2 * cols, rows), f32),
            pltpu.VMEM((slots, 2, 2 * xs, cols, rows), f32),
            pltpu.VMEM((2, cols, rows), f32),
            pltpu.VMEM((2 * xs, cols, rows), f32),
            pltpu.VMEM((cols, rows), f32),
            pltpu.VMEM((n, cols, 128), f32),
            dma((slots,)),
            dma((5,)),
            dma((slots, n, chunks)), dma((slots, n, chunks)),
            dma((slots, n)), dma((slots, n)),
            dma, dma,
            dma((slots, n, chunks)), dma((slots, n, chunks)),
            dma((slots, 2, chunks, 2 * xs)), dma((slots, 2, chunks, 2 * xs)),
            dma((2 * xs - 1,)), dma((2 * xs - 1,)),
            dma((n,)), dma((n,)),
        ],
        compiler_params=pltpu.CompilerParams(
            collective_id=0, has_side_effects=True, vmem_limit_bytes=63 * 1024 * 1024
        ),
    )(
        kernel_inverse_scale, view_weight, ridge_term, features, residual.T, direction.T,
    )
    product, step_size, ratio = product.T, step_size.T, ratio.T
    solution_next = solution + step_size * direction
    residual_next = residual - step_size * product
    direction_next = residual_next + ratio * direction
    return (solution_next, residual_next, direction_next)


def solution(mesh):
    return jax.shard_map(
        per_device,
        mesh=mesh,
        in_specs=(
            P("views", ("groups", "samples"), None),
            P(),
            P(),
            P("rhs"),
            P(("groups", "samples"), "rhs"),
            P(("groups", "samples"), "rhs"),
            P(("groups", "samples"), "rhs"),
        ),
        out_specs=(
            P(("groups", "samples"), "rhs"),
            P(("groups", "samples"), "rhs"),
            P(("groups", "samples"), "rhs"),
        ),
        check_vma=False,
    )
```

```python
import functools
import math

import jax
import jax.numpy as jnp
from jax import lax
from jax.experimental import pallas as pl
from jax.experimental.pallas import tpu as pltpu
from jax.sharding import PartitionSpec as P

MESH = pl.DeviceIdType.MESH
LANES = (((1,), (1,)), ((), ()))


def cg_kernel(
    n, slots, tile,
    scale_hbm, weight_hbm, ridge_hbm, feats_ref, res_hbm, dir_hbm,
    product_out, step_out, ratio_out,
    scale_ref, weight_ref, ridge_ref, res_ref,
    buf, dbuf, dpair, acc, ext_acc, norms, norms_end, cout, cin, late, part, gath, tot, stats,
    load_sem, small_sem, fs, fr, ds, dr, ps, pr, cs, cr, ls, lr, gs, gr, ss, sr,
):
    z = lax.axis_index("samples")
    x = lax.axis_index("views")
    c = lax.axis_index("rhs")
    xs = lax.axis_size("views")
    local_views = feats_ref.shape[0]
    first_view = x * local_views
    rows = feats_ref.shape[1]
    half = local_views // 2
    pieces = [pl.ds(k * tile, tile) for k in range(rows // tile)]

    if slots == 2:
        view = [c, half + c]
        sgn = [1, -1]
        pos = [z, n - 1 - z]
    else:
        view = [c]
        sgn = [1 - 2 * c]
        pos = [z * (1 - c) + (n - 1 - z) * c]

    def load(s):
        return pltpu.make_async_copy(feats_ref.at[view[s]], buf.at[s, 0], load_sem.at[s])

    fetch = [
        pltpu.make_async_copy(src, dst, small_sem.at[k])
        for k, (src, dst) in enumerate((
            (dir_hbm, dpair.at[c]), (scale_hbm, scale_ref), (weight_hbm, weight_ref),
            (ridge_hbm, ridge_ref), (res_hbm, res_ref),
        ))
    ]
    for s in range(slots):
        load(s).start()
    for copy in fetch:
        copy.start()

    barrier = pltpu.get_barrier_semaphore()
    sides = (z > 0).astype(jnp.int32) + (z < n - 1).astype(jnp.int32)
    cross = [(dx, dc) for dx in range(xs) for dc in range(2) if (dx, dc) != (0, 0)]
    for near, there in ((z - 1, z > 0), (z + 1, z < n - 1)):
        @pl.when(there)
        def _(near=near):
            pl.semaphore_signal(
                barrier, inc=1, device_id={"samples": near}, device_id_type=MESH)
    for dx, dc in cross:
        pl.semaphore_signal(
            barrier, inc=1, device_id_type=MESH,
            device_id={"views": lax.rem(x + dx, xs), "rhs": lax.rem(c + dc, 2)})

    def consts(s):
        index = first_view + view[s]
        rate = scale_ref[index] * math.log2(math.e)
        return rate, jnp.log2(jnp.full((1, 1), weight_ref[index], jnp.float32))

    def row_term(s, slot_ref, norms):
        rate, low_weight = consts(s)
        feats = slot_ref[...].astype(jnp.float32)
        sums = lax.dot_general(
            jnp.ones((8, feats.shape[1]), jnp.float32), feats * feats, LANES,
            precision=lax.Precision.HIGHEST, preferred_element_type=jnp.float32,
        )
        norms[s] = low_weight - rate * sums

    for copy in fetch:
        copy.wait()
    for s in range(slots):
        load(s).wait()
    pl.semaphore_wait(barrier, len(cross) + sides)

    def remote(src, dst, send, recv, target):
        return pltpu.make_async_remote_copy(
            src_ref=src, dst_ref=dst, send_sem=send, recv_sem=recv,
            device_id=target, device_id_type=MESH,
        )

    def ahead(s, steps):
        return {"samples": lax.rem(z + sgn[s] * steps + 2 * n, n)}

    def forward(s, d):
        return tuple(
            remote(buf.at[s, d, at], buf.at[s, d + 1, at],
                   fs.at[s, d, k], fr.at[s, d + 1, k], ahead(s, 1))
            for k, at in enumerate(pieces)
        ) + (
            remote(dbuf.at[s, d], dbuf.at[s, d + 1], ds.at[s, d], dr.at[s, d + 1], ahead(s, 1)),
        )

    def back(s):
        return tuple(
            remote(buf.at[s, 0, at], buf.at[s, n - 1, at],
                   fs.at[s, n - 1, k], fr.at[s, n - 1, k], ahead(s, -1))
            for k, at in enumerate(pieces)
        ) + (
            remote(dbuf.at[s, 0], dbuf.at[s, n - 1], ds.at[s, n - 1], dr.at[s, n - 1], ahead(s, -1)),
        )

    here = x * 2 + c
    owners = [(dx, oc) for dx in range(xs) for oc in range(2)]

    def give(s, d, k):
        return remote(cout.at[s, d, :, pieces[k]], cin.at[s, d, :, pieces[k]],
                      cs.at[s, d, k], cr.at[s, d, k], ahead(s, -d))

    def give_last(s, k):
        return [
            remote(cout.at[s, n - 2, pl.ds(8 * oc, 8), pieces[k]],
                   late.at[s, 0, here, :, pieces[k]],
                   ls.at[s, 0, k, j], lr.at[s, 0, k, here],
                   {"views": lax.rem(x + dx, xs), "rhs": oc} | ahead(s, 2 - n))
            for j, (dx, oc) in enumerate(owners)
        ]

    def give_end(s):
        return [
            remote(ext_acc.at[s, pl.ds(8 * oc, 8)], late.at[s, 1, here],
                   ls.at[s, 1, 0, j], lr.at[s, 1, 0, here],
                   {"views": lax.rem(x + dx, xs), "rhs": oc} | ahead(s, 1))
            for j, (dx, oc) in enumerate(owners)
        ]

    def taken(s, e, k, source):
        at = pl.ds(0, rows) if e else pieces[k]
        return remote(cout.at[s, n - 2, pl.ds(0, 8), at], late.at[s, e, source, :, at],
                      ls.at[s, e, k, 0], lr.at[s, e, k, source], ahead(s, 1))

    for s in range(slots):
        @pl.when(pos[s] < n - 1)
        def _(s=s):
            forward(s, 0)[0].start()

    pair = remote(dpair.at[c], dpair.at[c], ps, pr, {"rhs": 1 - c})
    pair.start()
    pair.wait_recv()
    low = jnp.concatenate([dpair[0], dpair[1]], axis=0).astype(jnp.bfloat16)
    for s in range(slots):
        dbuf[s, 0] = low

        @pl.when(pos[s] < n - 1)
        def _(s=s):
            forward(s, 0)[-1].start()
            for copy in forward(s, 0)[1:-1]:
                copy.start()

    def block(s, jb, ib, jd, at, i_sum, j_sum, add_j, norms):
        rate, _ = consts(s)
        fj = jb[at, :]
        inner = lax.dot_general(fj, ib[...], LANES, preferred_element_type=jnp.float32)
        wide = fj.astype(jnp.float32)
        column = -rate * jnp.sum(wide * wide, axis=-1, keepdims=True)
        power = (2.0 * rate) * inner + norms[s, 0:1, :] + column
        kern = jnp.exp2(power).astype(jnp.bfloat16)
        i_sum[...] += jnp.dot(jd[:, at], kern, preferred_element_type=jnp.float32)
        if j_sum is not None:
            (idir, target) = j_sum
            term = lax.dot_general(idir[...], kern, LANES, preferred_element_type=jnp.float32)
            if add_j:
                target[:, at] += term
            else:
                target[:, at] = term

    def each_piece(run):
        def step(t, _):
            run(pl.ds(pl.multiple_of(t * tile, tile), tile))
            return 0

        lax.fori_loop(0, rows // tile, step, 0)

    for s in range(slots):
        row_term(s, buf.at[s, 0], norms)
    acc[...] = jnp.zeros_like(acc)
    for s in range(slots):
        each_piece(functools.partial(
            lambda s, at: block(s, buf.at[s, 0], buf.at[s, 0], dbuf.at[s, 0], at, acc, None, False,
                                norms),
            s))

    for s in range(slots):
        @pl.when(pos[s] == n - 1)
        def _(s=s):
            moves = back(s)
            moves[-1].start()
            for k in range(len(pieces)):
                if slots == 2:
                    forward(1 - s, 0)[k].wait_send()
                moves[k].start()

    def end_piece(s, k):
        if k == 0:
            for copy in back(s):
                copy.wait_recv()
            row_term(s, buf.at[s, n - 1], norms_end)
            ext_acc[s] = jnp.zeros(ext_acc.shape[1:], jnp.float32)
        block(s, buf.at[s, n - 2], buf.at[s, n - 1], dbuf.at[s, n - 2], pieces[k], ext_acc.at[s],
              (dbuf.at[s, n - 1], cout.at[s, n - 2]), True, norms_end)
        for copy in give_last(s, k):
            copy.start()

    def turn(d, _):
        for k, at in enumerate(pieces):
            for s in range(slots):
                @pl.when(pos[s] >= d)
                def _(s=s, k=k):
                    forward(s, d - 1)[k].wait_recv()

                    @pl.when((pos[s] < n - 1) & (d < n - 2))
                    def _():
                        forward(s, d)[k].start()

                    if k == 0:
                        forward(s, d - 1)[-1].wait_recv()

                        @pl.when((pos[s] < n - 1) & (d < n - 2))
                        def _():
                            forward(s, d)[-1].start()

            for s in range(slots):
                @pl.when(pos[s] >= d)
                def _(s=s, k=k, at=at):
                    block(s, buf.at[s, d], buf.at[s, 0], dbuf.at[s, d], at, acc,
                          (dbuf.at[s, 0], cout.at[s, d]), False, norms)

                    @pl.when(d < n - 2)
                    def _():
                        give(s, d, k).start()

                    @pl.when((pos[s] == n - 1) & (d == n - 2))
                    def _():
                        for copy in give_last(s, k):
                            copy.start()

                    if k < len(pieces) - 1:
                        @pl.when((pos[s] == n - 2) & (d == n - 2))
                        def _():
                            end_piece(s, k)
        return 0

    lax.fori_loop(1, n - 1, turn, 0)

    def collect(d, _):
        for s in range(slots):
            @pl.when(pos[s] + d <= n - 1)
            def _(s=s):
                for k in range(len(pieces)):
                    give(s, d, k).wait_recv()
                acc[...] += cin[s, d]
        return 0

    lax.fori_loop(1, n - 2, collect, 0)

    part[0] = acc[0:8, :]
    part[1] = acc[8:16, :]

    def swap(k):
        dx, dc = cross[k]
        tx, tc = lax.rem(x + dx, xs), lax.rem(c + dc, 2)
        return remote(part.at[tc], gath.at[here], gs.at[k], gr.at[k], {"views": tx, "rhs": tc})

    for k in range(len(cross)):
        swap(k).start()
    gath[here] = part[c]

    for s in range(slots):
        @pl.when(pos[s] == n - 2)
        def _(s=s):
            end_piece(s, len(pieces) - 1)
            for copy in give_end(s):
                copy.start()


    def place(s, core):
        return pos[s] if slots == 2 else z * (1 - core) + (n - 1 - z) * core

    for k in range(len(cross)):
        swap(k).wait_recv()
    direction = dpair[c]
    residual = res_ref[...]
    summed = gath[0]
    for k in range(1, 2 * xs):
        summed = summed + gath[k]
    tot[...] = summed

    for s in range(slots):
        for core in range(2):
            for e in range(2):
                @pl.when((place(s, core) <= 1) if e == 0 else (place(s, core) == n - 1))
                def _(s=s, core=core, e=e):
                    for other in range(xs):
                        source = other * 2 + core
                        for k in range(1 if e else len(pieces)):
                            taken(s, e, k, source).wait_recv()
                        tot[...] += late[s, e, source]
    summed = tot[...]
    row = lax.broadcasted_iota(jnp.int32, (8, 1), 0)
    ridge = jnp.zeros((8, 1), jnp.float32)
    for k in range(8):
        ridge = jnp.where(row == k, ridge_ref[k], ridge)
    product = summed + ridge * direction
    product_out[...] = product

    def total(value):
        return jnp.sum(value, axis=-1, keepdims=True)

    lane = lax.broadcasted_iota(jnp.int32, (8, 128), 1)
    sums = jnp.zeros((8, 128), jnp.float32)
    for k, value in enumerate((residual * residual, direction * product,
                               residual * product, product * product)):
        sums = jnp.where(lane == k, total(value), sums)
    stats[z] = sums

    def spread(k):
        return remote(stats.at[z], stats.at[z], ss.at[k], sr.at[k], {"samples": lax.rem(z + k, n)})

    for k in range(1, n):
        spread(k).start()
    for k in range(1, n):
        spread(k).wait_recv()
    sums = stats[0]
    for k in range(1, n):
        sums = sums + stats[k]
    norm_now, curvature, cross_term, square = (sums[:, k:k + 1] for k in range(4))
    step_size = norm_now / curvature
    norm_next = jnp.maximum(norm_now - step_size * (2.0 * cross_term - step_size * square), 0.0)
    step_out[...] = jnp.broadcast_to(step_size, step_out.shape)
    ratio_out[...] = jnp.broadcast_to(norm_next / norm_now, ratio_out.shape)

    pair.wait_send()
    for k in range(len(cross)):
        swap(k).wait_send()
    for k in range(1, n):
        spread(k).wait_send()
    for s in range(slots):
        @pl.when(pos[s] < n - 1)
        def _(s=s):
            if slots == 2:
                @pl.when(pos[1 - s] != n - 1)
                def _():
                    for copy in forward(s, 0)[:-1]:
                        copy.wait_send()
            else:
                for copy in forward(s, 0)[:-1]:
                    copy.wait_send()
            forward(s, 0)[-1].wait_send()

        @pl.when(pos[s] == n - 1)
        def _(s=s):
            for copy in back(s):
                copy.wait_send()

        @pl.when(pos[s] == n - 2)
        def _(s=s):
            for copy in give_end(s):
                copy.wait_send()

    def drain(d, _):
        for s in range(slots):
            @pl.when(pos[s] >= d)
            def _(s=s):
                for k in range(len(pieces)):
                    @pl.when(d < n - 2)
                    def _(k=k):
                        give(s, d, k).wait_send()

                    @pl.when(d == n - 2)
                    def _(k=k):
                        for copy in give_last(s, k):
                            copy.wait_send()

                @pl.when((pos[s] < n - 1) & (d < n - 2))
                def _():
                    for copy in forward(s, d):
                        copy.wait_send()
        return 0

    lax.fori_loop(1, n - 1, drain, 0)


def per_device(
    features, kernel_inverse_scale, view_weight, ridge_term, solution, residual, direction
):
    n = lax.axis_size("samples")
    xs = lax.axis_size("views")
    local_views, rows, feat = features.shape
    cols = direction.shape[1]
    slots = local_views // 2
    tile = math.gcd(rows, 512)
    chunks = rows // tile
    vmem = pl.BlockSpec(memory_space=pltpu.VMEM)
    hbm = pl.BlockSpec(memory_space=pltpu.HBM)
    dma = pltpu.SemaphoreType.DMA
    f32, bf16 = jnp.float32, jnp.bfloat16
    out = jax.ShapeDtypeStruct((cols, rows), f32)
    product, step_size, ratio = pl.pallas_call(
        functools.partial(cg_kernel, n, slots, tile),
        out_shape=(out, out, out),
        in_specs=[hbm] * 6,
        out_specs=(vmem, vmem, vmem),
        scratch_shapes=[
            pltpu.SMEM(kernel_inverse_scale.shape, f32),
            pltpu.SMEM(view_weight.shape, f32),
            pltpu.SMEM(ridge_term.shape, f32),
            pltpu.VMEM((cols, rows), f32),
            pltpu.VMEM((slots, n, rows, feat), bf16),
            pltpu.VMEM((slots, n, 2 * cols, rows), bf16),
            pltpu.VMEM((2, cols, rows), f32),
            pltpu.VMEM((2 * cols, rows), f32),
            pltpu.VMEM((slots, 2 * cols, rows), f32),
            pltpu.VMEM((slots, 8, rows), f32),
            pltpu.VMEM((slots, 8, rows), f32),
            pltpu.VMEM((slots, n, 2 * cols, rows), f32),
            pltpu.VMEM((slots, n, 2 * cols, rows), f32),
            pltpu.VMEM((slots, 2, 2 * xs, cols, rows), f32),
            pltpu.VMEM((2, cols, rows), f32),
            pltpu.VMEM((2 * xs, cols, rows), f32),
            pltpu.VMEM((cols, rows), f32),
            pltpu.VMEM((n, cols, 128), f32),
            dma((slots,)),
            dma((5,)),
            dma((slots, n, chunks)), dma((slots, n, chunks)),
            dma((slots, n)), dma((slots, n)),
            dma, dma,
            dma((slots, n, chunks)), dma((slots, n, chunks)),
            dma((slots, 2, chunks, 2 * xs)), dma((slots, 2, chunks, 2 * xs)),
            dma((2 * xs - 1,)), dma((2 * xs - 1,)),
            dma((n,)), dma((n,)),
        ],
        compiler_params=pltpu.CompilerParams(
            collective_id=0, has_side_effects=True, vmem_limit_bytes=63 * 1024 * 1024
        ),
    )(
        kernel_inverse_scale, view_weight, ridge_term, features, residual.T, direction.T,
    )
    product, step_size, ratio = product.T, step_size.T, ratio.T
    solution_next = solution + step_size * direction
    residual_next = residual - step_size * product
    direction_next = residual_next + ratio * direction
    return (solution_next, residual_next, direction_next)


def solution(mesh):
    return jax.shard_map(
        per_device,
        mesh=mesh,
        in_specs=(
            P("views", ("groups", "samples"), None),
            P(),
            P(),
            P("rhs"),
            P(("groups", "samples"), "rhs"),
            P(("groups", "samples"), "rhs"),
            P(("groups", "samples"), "rhs"),
        ),
        out_specs=(
            P(("groups", "samples"), "rhs"),
            P(("groups", "samples"), "rhs"),
            P(("groups", "samples"), "rhs"),
        ),
        check_vma=False,
    )
```
